512 devices in a mesh: seq: 32 (over z, core), tp: 4 (over y), dp: 4 (over x).
Axes of the slice: x: 4, y: 4, z: 16, core: 2. Of those that a mesh axis runs over, the one named last changes fastest.
Arguments:
- queries: bfloat16 [4, 8192, 2048], P(None, 'seq', ('tp', 'dp')), may hold values from -64 to 64
- block_states: bfloat16 [4, 8192, 2048], P(None, 'seq', ('tp', 'dp')), may hold values from -40 to 40
- grad_out: bfloat16 [4, 8192, 2048], P(None, 'seq', ('tp', 'dp')), may hold values from -6 to 6
- store: bfloat16 [1024, 128, 2048], P('seq', None, ('tp', 'dp')), may hold values from -40 to 40
- owners: int32 [128, 4, 2], P('seq'), may hold values from 0 to 31, all different within a row; in each aligned block of 16 rows (0 to 15, 16 to 31, ..., all dimensions but the last counted through in order) at most 2 rows name the same one
- entries: int32 [128, 4, 2], P('seq'), may hold values from 0 to 31
Outputs:
- attended: bfloat16 [4, 8192, 2048], P(None, 'seq', ('tp', 'dp'))
- query_grad: bfloat16 [4, 8192, 2048], P(None, 'seq', ('tp', 'dp'))
- state_grad: bfloat16 [4, 8192, 2048], P(None, 'seq', ('tp', 'dp'))
The draws below stay inside these ranges and needn't reach their ends.
Inputs may be any that keep to these rules, and one draw needn't show every extreme that they name: Within the rows of one device (aligned blocks of 16 rows), no owner is named more than 2 times, a bound that some block reaches; the 2 neighbours of a block name different owners.
All inputs are finite; a program needn't handle non-finite values.
Results may differ from the reference program's by a relative error of at most 0.01295.
Values may be sent and summed in bfloat16 or wider, within the bound.
A program may use at most 64 MiB of HBM per device.

```python
import math
import jax
import jax.numpy as jnp
import numpy as np
from jax import lax

DE = 2048
HEADS = 16
HD = 128
BLOCK = 64
NLEN = 128
NBR = 2
SEQS = 4
BLK_DEV = 4
DB_DEV = 32
BLOCKS = 128
LEN = 8192
STORE_ROWS = 1024
SLOT = 2
N_SEQ = 32


def draw_store(key, part):
    key = jax.random.fold_in(key, 1)
    shape = (STORE_ROWS, NLEN, DE)
    values = jax.random.normal(key, shape, jnp.float32)
    return jnp.clip(values, -40.0, 40.0).astype(jnp.bfloat16)


def draw_block_states(key, part):
    key = jax.random.fold_in(key, 2)
    shape = (SEQS, LEN, DE)
    values = jax.random.normal(key, shape, jnp.float32)
    return jnp.clip(values, -40.0, 40.0).astype(jnp.bfloat16)


def draw_queries(key, part):
    key = jax.random.fold_in(key, 3)
    shape = (SEQS, LEN, DE)
    values = jax.random.normal(key, shape, jnp.float32)
    return jnp.clip(values, -64.0, 64.0).astype(jnp.bfloat16)


def with_ends(values, key, smallest, top_value):
    index_at = [jax.random.randint(jax.random.fold_in(key, axis), (), 0, length) for axis, length in enumerate(values.shape)]
    widest = values.shape.index(max(values.shape))
    neighbour = index_at[:widest] + [(index_at[widest] + 1) % values.shape[widest]] + index_at[widest + 1:]
    return values.at[tuple(index_at)].set(smallest).at[tuple(neighbour)].set(top_value)


def shard_levels(own_key, dims, cuts, smallest, largest):
    def one(axis_at, parts):
        draws = jax.random.uniform(jax.random.fold_in(jax.random.fold_in(own_key, 6), axis_at), (parts,), jnp.float32, smallest / len(cuts), largest / len(cuts))
        return jnp.repeat(jnp.exp(draws), dims[axis_at] // parts).reshape((-1,) + (1,) * (len(dims) - axis_at - 1))

    level = one(*cuts[0])
    for cut in cuts[1:]:
        level = level * one(*cut)
    return level


def routed_block(own_key, own, number, rows, amount, top, most, slope):
    ranking = jax.random.permutation(own_key, amount)
    heavy_load, common = shares(amount, rows * top, most, slope, True), shares(amount, rows * top, most, slope, False)
    places = jnp.arange(amount)

    def named(lengths, rotation):
        used = int((lengths > 0).sum())
        fixed = max(1, used // 4)
        moved = fixed + (places - fixed + rotation * (used - fixed)) % max(1, amount - fixed)
        return jnp.zeros((amount,), jnp.int32).at[ranking[jnp.where(places < fixed, places, moved)]].set(jnp.asarray(lengths, jnp.int32))

    lengths = jnp.where(number % 4 == 0, named(heavy_load, number // 4), named(common, number - number // 4 - 1))
    mixed = jax.random.permutation(jax.random.fold_in(own, 3), amount)
    source_of, sink = mixed[0:amount // 2 * 2:2], mixed[1:amount // 2 * 2:2]
    slack = jnp.minimum(lengths[source_of] - 1, most - lengths[sink]) // 2
    slack = jnp.where((source_of == ranking[0]) | (sink == ranking[0]) | (lengths[sink] == 0), 0, jnp.maximum(slack, 0))
    moved = jax.random.randint(jax.random.fold_in(own, 4), (amount // 2,), 0, 1 << 20) % (slack + 1)
    lengths = lengths.at[source_of].add(-moved).at[sink].add(moved)
    members = jnp.searchsorted(jnp.cumsum(lengths), jnp.arange(rows * top), side="right").astype(jnp.int32)
    table = members.reshape(top, rows).T
    table = table[jax.random.permutation(jax.random.fold_in(own, 1), rows)]
    rotation = jax.random.randint(jax.random.fold_in(own, 2), (rows, 1), 0, top)
    return jnp.take_along_axis(table, (jnp.arange(top)[None, :] + rotation) % top, axis=1)


def shares(count, total, most, slope, full):
    loads = [(1 << 20) // math.isqrt(grade ** slope) + 1 for grade in range(1, count + 1)]
    largest = most if full else min(most, max(-(-total // count), total * loads[0] // sum(loads)))
    least = 1 if total - largest >= count - 1 else 0
    given, surplus = [largest] + [least] * (count - 1), total - largest - least * (count - 1)
    while surplus > 0:
        movable = [i for i in range(1, count) if given[i] < largest] or [i for i in range(1, count) if given[i] < most]
        mass, budget = sum([loads[i] for i in movable]), surplus
        for i in movable:
            extra = min(most - given[i], max(1, budget * loads[i] // mass), surplus)
            given[i] = given[i] + extra
            surplus = surplus - extra
    return np.array(given)


def scatter_about(own_key, dims, scale, bound, cuts=(), kind=jnp.bfloat16):
    drawn = jax.random.normal(own_key, dims, jnp.float32) * scale
    if len(cuts) > 0:
        drawn = shard_levels(own_key, dims, cuts, -0.22, 0.18) * drawn
    return jnp.clip(drawn, min=-bound, max=bound).astype(kind)


def setup_inputs(seed: int = 0) -> dict:
    key_of = jax.random.split(jax.random.key(seed), 7)
    queries = draw_queries(jax.random.fold_in(key_of[6], 71), 0)
    block_states = draw_block_states(jax.random.fold_in(key_of[6], 71), 0)
    grad_out = scatter_about(key_of[2], (SEQS, LEN, DE), 1.0, 6.0, ((1, 32), (2, 16)))
    store = draw_store(jax.random.fold_in(key_of[6], 71), 0)
    owners_keys = jax.random.split(jax.random.fold_in(key_of[4], 1), BLOCKS * SEQS // (BLK_DEV * SEQS))
    owners_turns = jax.random.permutation(jax.random.fold_in(key_of[4], 3), BLOCKS * SEQS // (BLK_DEV * SEQS))
    owners = jax.vmap(lambda own, number: routed_block(jax.random.fold_in(key_of[4], 2), own, number, BLK_DEV * SEQS, N_SEQ, NBR, SLOT, 2))(owners_keys, owners_turns).reshape((BLOCKS, SEQS, NBR))
    entries = with_ends(jax.random.randint(key_of[5], (BLOCKS, SEQS, NBR), 0, DB_DEV), jax.random.fold_in(key_of[5], 1), 0, DB_DEV - 1).astype(jnp.int32)
    return {"queries": queries, "block_states": block_states, "grad_out": grad_out, "store": store, "owners": owners, "entries": entries}


norm_eps = 1e-06

def softmax_rows(scores):
    row_top = lax.optimization_barrier(jnp.max(scores, axis=-1, keepdims=True))
    raised = jnp.exp(scores - row_top)
    return raised / lax.optimization_barrier(jnp.sum(raised, axis=-1, keepdims=True))

def round_low(values):
    return lax.optimization_barrier(values.astype(jnp.bfloat16)).astype(jnp.float32)

def encode_rows(neighbours, states, score_scale):
    nbr_full = neighbours.astype(jnp.float32)
    state_full = states.astype(jnp.float32)
    scores = jnp.einsum('...qhd,...khd->...hqk', nbr_full, state_full) * score_scale
    weights = softmax_rows(scores)
    low_weights = round_low(weights)
    mixture = jnp.einsum('...hqk,...khd->...qhd', low_weights, state_full)
    summed = nbr_full + mixture
    squares = lax.optimization_barrier(jnp.sum(summed * summed, axis=(-2, -1)))
    inverse = lax.rsqrt(squares / DE + norm_eps)[..., None, None]
    normed = summed * inverse
    return (normed.astype(jnp.bfloat16), weights, low_weights, normed, inverse)

def encode_grads(neighbours, states, grad_rows, weights, low_weights, normed, inverse, score_scale):
    grad_full = grad_rows.astype(jnp.float32)
    projection = lax.optimization_barrier(jnp.sum(grad_full * normed, axis=(-2, -1)))[..., None, None]
    summed_grad = round_low(inverse * (grad_full - normed * (projection / DE)))
    state_full = states.astype(jnp.float32)
    weight_grad = jnp.einsum('...qhd,...khd->...hqk', summed_grad, state_full)
    score_grad = round_low(weights * (weight_grad - lax.optimization_barrier(jnp.sum(weight_grad * weights, axis=-1, keepdims=True))))
    state_term = jnp.einsum('...hqk,...qhd->...khd', low_weights, summed_grad)
    state_term = state_term + score_scale * jnp.einsum('...hqk,...qhd->...khd', score_grad, neighbours.astype(jnp.float32))
    return state_term.astype(jnp.bfloat16)

def place_tokens(blocks, batch_seqs, length, columns):
    ordered = jnp.transpose(blocks, (1, 0, 2, 3)).reshape(batch_seqs, length, columns)
    leading = jnp.zeros((batch_seqs, BLOCK - 1, columns), blocks.dtype)
    return jnp.concatenate([leading, ordered[:, :length - BLOCK + 1]], axis=1)

def reference(queries, block_states, grad_out, store, owners, entries):
    batch_seqs, length, columns = queries.shape
    score_scale = HD ** (-0.5)
    padding = ((0, 0), (1, BLOCK - 1), (0, 0))
    query_pad = jnp.pad(queries, padding)
    grad_pad = jnp.pad(grad_out, padding)

    def one_block(block_index):
        offset = block_index * BLOCK
        states = lax.dynamic_slice_in_dim(block_states, offset, BLOCK, 1).reshape(batch_seqs, 1, BLOCK, HEADS, HD)
        states = jnp.broadcast_to(states, (batch_seqs, NBR, BLOCK, HEADS, HD))
        picked = owners[block_index] * DB_DEV + entries[block_index]
        neighbours = store[picked].reshape(batch_seqs, NBR, NLEN, HEADS, HD)
        encoded, enc_weights, enc_low, normed, inverse = encode_rows(neighbours, states, score_scale)
        key_rows = lax.optimization_barrier(encoded).astype(jnp.float32).reshape(batch_seqs, NBR * NLEN, HEADS, HD)
        query_rows = lax.dynamic_slice_in_dim(query_pad, offset + BLOCK, BLOCK, 1).reshape(batch_seqs, BLOCK, HEADS, HD).astype(jnp.float32)
        grad_rows = lax.dynamic_slice_in_dim(grad_pad, offset + BLOCK, BLOCK, 1).reshape(batch_seqs, BLOCK, HEADS, HD).astype(jnp.float32)
        scores = jnp.einsum('bqhd,bkhd->bhqk', query_rows, key_rows) * score_scale
        weights = softmax_rows(scores)
        low_weights = round_low(weights)
        attended = jnp.einsum('bhqk,bkhd->bqhd', low_weights, key_rows).astype(jnp.bfloat16)
        weight_grad = jnp.einsum('bqhd,bkhd->bhqk', grad_rows, key_rows)
        score_grad = round_low(weights * (weight_grad - lax.optimization_barrier(jnp.sum(weight_grad * weights, axis=-1, keepdims=True))))
        query_grad = (score_scale * jnp.einsum('bhqk,bkhd->bqhd', score_grad, key_rows)).astype(jnp.bfloat16)
        key_grad = jnp.einsum('bhqk,bqhd->bkhd', low_weights, grad_rows)
        key_grad = key_grad + score_scale * jnp.einsum('bhqk,bqhd->bkhd', score_grad, query_rows)
        encoded_grad = key_grad.astype(jnp.bfloat16).reshape(batch_seqs, NBR, NLEN, HEADS, HD)
        state_term = encode_grads(neighbours, states, encoded_grad, enc_weights, enc_low, normed, inverse, score_scale)
        state_grad = lax.optimization_barrier(jnp.sum(state_term.astype(jnp.float32), axis=1)).astype(jnp.bfloat16)
        return (attended.reshape(batch_seqs, BLOCK, columns), query_grad.reshape(batch_seqs, BLOCK, columns), state_grad.reshape(batch_seqs, BLOCK, columns))
    attended_blocks, query_blocks, state_blocks = lax.map(one_block, jnp.arange(BLOCKS, dtype=jnp.int32))
    attended = place_tokens(attended_blocks, batch_seqs, length, columns)
    query_grad = place_tokens(query_blocks, batch_seqs, length, columns)
    state_grad = jnp.transpose(state_blocks, (1, 0, 2, 3)).reshape(batch_seqs, length, columns)
    return (attended, query_grad, state_grad)
```

```python
import functools

import jax
import jax.numpy as jnp
from jax import lax
from jax.experimental import pallas as pl
from jax.experimental.pallas import tpu as pltpu
from jax.sharding import PartitionSpec as P

HD = 128
BLOCK = 64
NLEN = 128
NBR = 2
SLOTS = 2
norm_eps = 1e-06
MESH = pl.DeviceIdType.MESH
f32 = jnp.float32
bf16 = jnp.bfloat16


def place_distance(place, members):
    turn = members // 2 + (place // 2) * (1 - 2 * ((place + 1) % 2))
    return turn


def nn(a, b):
    return lax.dot_general(a, b, (((1,), (0,)), ((), ())), preferred_element_type=f32)


def nt(a, b):
    return lax.dot_general(a, b, (((1,), (1,)), ((), ())), preferred_element_type=f32)


def shift_matrix(rows, columns, offset):
    i = lax.broadcasted_iota(jnp.int32, (rows, columns), 0)
    j = lax.broadcasted_iota(jnp.int32, (rows, columns), 1)
    return (j == i + offset).astype(f32).astype(bf16)


def kernel(
    members, ntp, ndp, seqs, groups, chunk,
    item_slot, slot_block, own_ids, ids_ref, q_ref, g_ref, s_ref, store_ref,
    att_ref, qg_ref, sg_ref,
    ids_in, ids_s, send, recv, summed, wts, squares, inv, qn, gn, qb, gb, qt, gt, st, atb, qgb, kgrad, proj,
    ids_send, ids_recv, loc_sem, tok_send, tok_recv, data_send, data_recv, sq_send, sq_recv, pr_send, pr_recv,
    o_send, o_recv,
):
    me = lax.axis_index("seq")
    tp = lax.axis_index("tp")
    dp = lax.axis_index("dp")
    peers = ntp * ndp
    scale = HD ** (-0.5)
    width = HD * peers
    after = lax.rem(me + 1, members)
    before = lax.rem(me + members - 1, members)

    def ring(distance):
        return {"seq": lax.rem(me + distance, members)}

    def plane(q):
        return {"tp": lax.rem(tp + q // ndp, ntp), "dp": lax.rem(dp + q % ndp, ndp)}

    barrier = pltpu.get_barrier_semaphore()

    def greet_ring(d, c):
        pl.semaphore_signal(barrier, inc=1, device_id=ring(d), device_id_type=MESH)
        return c

    def greet_plane(q, c):
        pl.semaphore_signal(barrier, inc=1, device_id=plane(q), device_id_type=MESH)
        return c

    lax.fori_loop(1, members, greet_ring, 0)
    lax.fori_loop(1, peers, greet_plane, 0)
    pl.semaphore_wait(barrier, members - 1 + peers - 1)

    def send_ids(d, c):
        pltpu.make_async_remote_copy(
            src_ref=ids_ref, dst_ref=ids_in.at[d], send_sem=ids_send, recv_sem=ids_recv,
            device_id=ring(d), device_id_type=MESH,
        ).start()
        return c

    lax.fori_loop(1, members, send_ids, 0)
    tok_copies = []
    for k, (src, dst) in enumerate(((q_ref, qn), (g_ref, gn))):
        copy = pltpu.make_async_remote_copy(
            src_ref=src.at[:, pl.ds(0, BLOCK)], dst_ref=dst, send_sem=tok_send.at[k], recv_sem=tok_recv.at[k],
            device_id={"seq": before}, device_id_type=MESH,
        )
        copy.start()
        tok_copies.append(copy)

    eye = shift_matrix(HD, HD, 0)

    for k in range(SLOTS):
        recv[k] = store_ref[own_ids[k]]

    def turn_states(i, c):
        st[i] = nt(eye, s_ref[i]).astype(bf16)
        return c

    lax.fori_loop(0, seqs * groups, turn_states, 0)

    pltpu.make_async_copy(ids_in.at[pl.ds(1, members - 1)], ids_in.at[pl.ds(1, members - 1)], ids_recv).wait()
    to_scalar = pltpu.make_async_copy(ids_in.at[pl.ds(1, members - 1)], ids_s.at[pl.ds(1, members - 1)], loc_sem)
    to_scalar.start()
    to_scalar.wait()

    def send_items(p, c):
        d = place_distance(p, members)
        for k in range(SLOTS):
            send[SLOTS * p + k] = store_ref[ids_s[members - d, 0, SLOTS * p + k]]
        pltpu.make_async_remote_copy(
            src_ref=send.at[pl.ds(SLOTS * p, SLOTS)], dst_ref=recv.at[pl.ds(SLOTS * p, SLOTS)],
            send_sem=data_send, recv_sem=data_recv.at[p], device_id=ring(d), device_id_type=MESH,
        ).start()
        return c

    lax.fori_loop(1, members, send_items, 0)

    for copy in tok_copies:
        copy.wait()
    last = (me < members - 1).astype(f32)
    first = (me > 0).astype(f32)
    for b in range(seqs):
        qn[b] = (qn[b].astype(f32) * last).astype(bf16)
        gn[b] = (gn[b].astype(f32) * last).astype(bf16)
    take = shift_matrix(BLOCK, 2 * BLOCK, BLOCK - 1)
    for b in range(seqs):
        for g in range(groups):
            i = b * groups + g
            for src, nxt, flat, turned in ((q_ref, qn, qb, qt), (g_ref, gn, gb, gt)):
                if g < groups - 1:
                    rows = src[b, pl.ds(BLOCK * g, 2 * BLOCK)]
                else:
                    rows = jnp.concatenate([src[b, pl.ds(BLOCK * g, BLOCK)], nxt[b]], axis=0)
                block = nn(take, rows).astype(bf16)
                flat[i] = block
                turned[i] = nt(eye, block).astype(bf16)

    def encode(slot, row):
        block = slot_block[slot]
        rows = recv[slot]
        scores = nt(s_ref[block], rows) * scale
        top = jnp.max(scores, axis=0, keepdims=True)
        raised = jnp.exp(scores - top)
        weights = raised / jnp.sum(raised, axis=0, keepdims=True)
        total = nn(st[block], weights.astype(bf16)) + nt(eye, rows)
        wts[slot] = weights
        summed[slot] = total
        squares[row[0], 0, pl.ds(row[1], 1), :] = jnp.sum(total * total, axis=0, keepdims=True)

    chunks = members // chunk
    rows_chunk = chunk * SLOTS

    def send_squares(c):
        def one(q, x):
            pltpu.make_async_remote_copy(
                src_ref=squares.at[c, 0], dst_ref=squares.at[c, q], send_sem=sq_send, recv_sem=sq_recv.at[c],
                device_id=plane(q), device_id_type=MESH,
            ).start()
            return x
        lax.fori_loop(1, peers, one, 0)

    for k in range(SLOTS):
        encode(k, (0, k))

    def encode_chunk(c, x):
        def one(p, y):
            pltpu.make_async_copy(
                recv.at[pl.ds(SLOTS * p, SLOTS)], recv.at[pl.ds(SLOTS * p, SLOTS)], data_recv.at[p]
            ).wait()
            for k in range(SLOTS):
                encode(SLOTS * p + k, (c, SLOTS * (p - c * chunk) + k))
            return y
        lax.fori_loop(jnp.maximum(c * chunk, 1), (c + 1) * chunk, one, 0)
        send_squares(c)
        return x

    lax.fori_loop(0, chunks, encode_chunk, 0)

    def finish_squares(c, x):
        pltpu.make_async_copy(
            squares.at[c, pl.ds(1, peers - 1)], squares.at[c, pl.ds(1, peers - 1)], sq_recv.at[c]
        ).wait()
        total = jnp.sum(squares[c], axis=0)
        inv[pl.ds(rows_chunk * c, rows_chunk), :] = lax.rsqrt(total / width + norm_eps)
        return x

    lax.fori_loop(0, chunks, finish_squares, 0)

    def attend(b, g):
        i = b * groups + g
        item = (g * seqs + b) * NBR
        normed = []
        for n in range(NBR):
            slot = item_slot[item + n]
            normed.append(summed[slot] * inv[pl.ds(slot, 1), :])
        normed = jnp.concatenate(normed, axis=1)
        keys = normed.astype(bf16)
        scores = nn(qb[i], keys) * scale
        raised = jnp.exp(scores - jnp.max(scores, axis=1, keepdims=True))
        weights = raised / jnp.sum(raised, axis=1, keepdims=True)
        low = weights.astype(bf16)
        atb[g + 1, b] = nt(low, keys).astype(bf16)
        wgrad = nn(gb[i], keys)
        slow = (weights * (wgrad - jnp.sum(weights * wgrad, axis=1, keepdims=True))).astype(bf16)
        qgb[g + 1, b] = (scale * nt(slow, keys)).astype(bf16)
        grad = (nn(gt[i], low) + scale * nn(qt[i], slow)).astype(bf16)
        kgrad[i] = grad
        inner = jnp.sum(grad.astype(f32) * normed, axis=0, keepdims=True)
        for n in range(NBR):
            proj[g, 0, pl.ds(NBR * b + n, 1), :] = inner[:, n * NLEN:(n + 1) * NLEN]

    def encode_grad(b, g):
        i = b * groups + g
        item = (g * seqs + b) * NBR
        total = None
        for n in range(NBR):
            slot = item_slot[item + n]
            scaled = inv[pl.ds(slot, 1), :]
            row = jnp.sum(proj[g, :, NBR * b + n, :], axis=0, keepdims=True) / width
            grad = kgrad[i, :, pl.ds(n * NLEN, NLEN)].astype(f32)
            sgrad = (scaled * (grad - summed[slot] * scaled * row)).astype(bf16)
            weights = wts[slot]
            wgrad = nn(s_ref[i], sgrad)
            slow = (weights * (wgrad - jnp.sum(weights * wgrad, axis=0, keepdims=True))).astype(bf16)
            term = nt(weights.astype(bf16), sgrad) + scale * nn(slow, recv[slot])
            term = term.astype(bf16).astype(f32)
            total = term if total is None else total + term
        sg_ref[b, pl.ds(g * BLOCK, BLOCK)] = total.astype(bf16)

    order = [groups - 1] + list(range(groups - 1))
    o_copies = []
    for g in order:
        for b in range(seqs):
            attend(b, g)
        if g == groups - 1:
            for k, buf in enumerate((atb, qgb)):
                copy = pltpu.make_async_remote_copy(
                    src_ref=buf.at[groups], dst_ref=buf.at[0], send_sem=o_send.at[k], recv_sem=o_recv.at[k],
                    device_id={"seq": after}, device_id_type=MESH,
                )
                copy.start()
                o_copies.append(copy)

        def send_proj(q, x, g=g):
            pltpu.make_async_remote_copy(
                src_ref=proj.at[g, 0], dst_ref=proj.at[g, q], send_sem=pr_send, recv_sem=pr_recv.at[g],
                device_id=plane(q), device_id_type=MESH,
            ).start()
            return x

        lax.fori_loop(1, peers, send_proj, 0)

    for g in order:
        pltpu.make_async_copy(
            proj.at[g, pl.ds(1, peers - 1)], proj.at[g, pl.ds(1, peers - 1)], pr_recv.at[g]
        ).wait()
        for b in range(seqs):
            encode_grad(b, g)

    for copy in o_copies:
        copy.wait()
    back = shift_matrix(BLOCK, 2 * BLOCK, 1)
    for buf, out in ((atb, att_ref), (qgb, qg_ref)):
        for b in range(seqs):
            buf[0, b] = (buf[0, b].astype(f32) * first).astype(bf16)
        for g in range(groups):
            for b in range(seqs):
                rows = jnp.concatenate([buf[g, b], buf[g + 1, b]], axis=0)
                out[b, pl.ds(g * BLOCK, BLOCK)] = nn(back, rows).astype(bf16)

    pltpu.make_async_copy(ids_in.at[pl.ds(1, members - 1)], ids_in.at[pl.ds(1, members - 1)], ids_send).wait()
    pltpu.make_async_copy(
        send.at[pl.ds(SLOTS, SLOTS * (members - 1))], send.at[pl.ds(SLOTS, SLOTS * (members - 1))], data_send
    ).wait()
    whole = squares.at[pl.ds(0, chunks), pl.ds(1, peers - 1)]
    pltpu.make_async_copy(whole, whole, sq_send).wait()
    whole = proj.at[pl.ds(0, groups), pl.ds(1, peers - 1)]
    pltpu.make_async_copy(whole, whole, pr_send).wait()


def on_device(members, ntp, ndp, queries, block_states, grad_out, store, owners, entries):
    seqs, rows, columns = queries.shape
    groups = rows // BLOCK
    blocks = seqs * groups
    items = blocks * NBR
    peers = ntp * ndp
    me = lax.axis_index("seq")
    flat_owner = owners.reshape(items)
    flat_entry = entries.reshape(items)

    distance = (me - flat_owner + members) % members
    half = members // 2
    step = distance - half
    place = jnp.where(step > 0, 2 * step + 1, jnp.where(step == 0, 1, -2 * step))
    place = jnp.where(distance == 0, 0, place)
    number = jnp.arange(items, dtype=jnp.int32)
    same = (flat_owner[:, None] == flat_owner[None, :]) & (number[None, :] < number[:, None])
    item_slot = place * SLOTS + jnp.sum(same.astype(jnp.int32), axis=1)
    cells = jnp.arange(members * SLOTS, dtype=jnp.int32)
    held = cells[:, None] == item_slot[None, :]
    slot_ids = jnp.sum(jnp.where(held, flat_entry[None, :], 0), axis=1)
    pair = number // NBR
    block_index = (pair % seqs) * groups + pair // seqs
    slot_block = jnp.sum(jnp.where(held, block_index[None, :], 0), axis=1)
    ids_row = jnp.pad(slot_ids, (0, 128 - members * SLOTS)).reshape(1, 128)

    chunk = max(1, members // 4)
    chunks = members // chunk
    vmem, smem = pltpu.VMEM, pltpu.SMEM
    dma = pltpu.SemaphoreType.DMA
    in_vmem = pl.BlockSpec(memory_space=vmem)
    in_smem = pl.BlockSpec(memory_space=smem)
    out = jax.ShapeDtypeStruct((seqs, rows, columns), bf16)
    attended, query_grad, state_grad = pl.pallas_call(
        functools.partial(kernel, members, ntp, ndp, seqs, groups, chunk),
        out_shape=(out, out, out),
        in_specs=[in_smem] * 3 + [in_vmem] * 5,
        out_specs=(in_vmem,) * 3,
        scratch_shapes=[
            vmem((members, 1, 128), jnp.int32),
            smem((members, 1, 128), jnp.int32),
            vmem((members * SLOTS, NLEN, HD), bf16),
            vmem((members * SLOTS, NLEN, HD), bf16),
            vmem((members * SLOTS, HD, NLEN), f32),
            vmem((members * SLOTS, BLOCK, NLEN), f32),
            vmem((chunks, peers, chunk * SLOTS, NLEN), f32),
            vmem((members * SLOTS, NLEN), f32),
            vmem((seqs, BLOCK, HD), bf16),
            vmem((seqs, BLOCK, HD), bf16),
            vmem((blocks, BLOCK, HD), bf16),
            vmem((blocks, BLOCK, HD), bf16),
            vmem((blocks, HD, BLOCK), bf16),
            vmem((blocks, HD, BLOCK), bf16),
            vmem((blocks, HD, BLOCK), bf16),
            vmem((groups + 1, seqs, BLOCK, HD), bf16),
            vmem((groups + 1, seqs, BLOCK, HD), bf16),
            vmem((blocks, HD, NBR * NLEN), bf16),
            vmem((groups, peers, seqs * NBR, NLEN), f32),
            dma, dma, dma, dma((2,)), dma((2,)),
            dma, dma((members,)), dma, dma((chunks,)), dma, dma((groups,)),
            dma((2,)), dma((2,)),
        ],
        compiler_params=pltpu.CompilerParams(
            collective_id=0, has_side_effects=True, vmem_limit_bytes=40 * 1024 * 1024
        ),
    )(
        item_slot, slot_block, slot_ids, ids_row, queries, grad_out,
        block_states.reshape(blocks, BLOCK, columns), store,
    )
    return attended, query_grad, state_grad


def solution(mesh):
    members, ntp, ndp = (mesh.shape[a] for a in ("seq", "tp", "dp"))
    rows = P(None, "seq", ("tp", "dp"))
    return jax.shard_map(
        functools.partial(on_device, members, ntp, ndp),
        mesh=mesh,
        in_specs=(rows, rows, rows, P("seq", None, ("tp", "dp")), P("seq", None, None), P("seq", None, None)),
        out_specs=(rows, rows, rows),
        check_vma=False,
    )
```

```python
import functools

import jax
import jax.numpy as jnp
from jax import lax
from jax.experimental import pallas as pl
from jax.experimental.pallas import tpu as pltpu
from jax.sharding import PartitionSpec as P

HD = 128
BLOCK = 64
NLEN = 128
NBR = 2
SLOTS = 2
norm_eps = 1e-06
MESH = pl.DeviceIdType.MESH
f32 = jnp.float32
bf16 = jnp.bfloat16


def near_places(members):
    return min(10, (members // 4) * 2)


def near_distance(place, members):
    return members + ((place + 1) // 2) * (1 - 2 * ((place + 1) % 2))


def far_distance(place, members):
    step = place - 1 - near_places(members)
    return members // 2 + ((step + 1) // 2) * (1 - 2 * (step % 2))


def nn(a, b):
    return lax.dot_general(a, b, (((1,), (0,)), ((), ())), preferred_element_type=f32)


def nt(a, b):
    return lax.dot_general(a, b, (((1,), (1,)), ((), ())), preferred_element_type=f32)


def shift_matrix(rows, columns, offset):
    i = lax.broadcasted_iota(jnp.int32, (rows, columns), 0)
    j = lax.broadcasted_iota(jnp.int32, (rows, columns), 1)
    return (j == i + offset).astype(f32).astype(bf16)


def kernel(
    members, ntp, ndp, seqs, groups, chunk,
    item_slot, slot_block, own_ids, ids_ref, q_hbm, g_hbm, s_hbm, store_hbm,
    att_ref, qg_ref, sg_ref,
    q_ref, g_ref, s_ref, store_ref, ids_in, ids_s, send, recv, summed, ukeys, sraw, wraw, wts, squares, inv, qn, gn, qb, gb, qt, gt, st, kblk, atb, qgb, kgrad, proj,
    in_sem, ids_send, ids_recv, loc_sem, tok_send, tok_recv, data_send, data_recv, sq_send, sq_recv, pr_send, pr_recv,
    o_send, o_recv,
):
    me = lax.axis_index("seq")
    tp = lax.axis_index("tp")
    dp = lax.axis_index("dp")
    peers = ntp * ndp
    scale = HD ** (-0.5)
    width = HD * peers
    after = lax.rem(me + 1, members)
    before = lax.rem(me + members - 1, members)

    def ring(distance):
        return {"seq": lax.rem(me + distance, members)}

    def plane(q):
        return {"tp": lax.rem(tp + q // ndp, ntp), "dp": lax.rem(dp + q % ndp, ndp)}

    barrier = pltpu.get_barrier_semaphore()

    def greet_ring(d, c):
        pl.semaphore_signal(barrier, inc=1, device_id=ring(d), device_id_type=MESH)
        return c

    def greet_plane(q, c):
        pl.semaphore_signal(barrier, inc=1, device_id=plane(q), device_id_type=MESH)
        return c

    lax.fori_loop(1, members, greet_ring, 0)
    lax.fori_loop(1, peers, greet_plane, 0)
    loads = []
    for k, (src, dst) in enumerate(((store_hbm, store_ref), (s_hbm, s_ref), (q_hbm, q_ref), (g_hbm, g_ref))):
        load = pltpu.make_async_copy(src, dst, in_sem.at[k])
        load.start()
        loads.append(load)
    pl.semaphore_wait(barrier, members - 1 + peers - 1)

    near = near_places(members)
    parts = ((1, near + 1, near_distance), (near + 1, members, far_distance))
    for k, (low, high, distance) in enumerate(parts):
        def send_ids(p, c, k=k, distance=distance):
            pltpu.make_async_remote_copy(
                src_ref=ids_ref, dst_ref=ids_in.at[p], send_sem=ids_send, recv_sem=ids_recv.at[k],
                device_id=ring(2 * members - distance(p, members)), device_id_type=MESH,
            ).start()
            return c

        lax.fori_loop(low, high, send_ids, 0)
    tok_copies = []
    for k, (src, dst) in enumerate(((q_hbm, qn), (g_hbm, gn))):
        copy = pltpu.make_async_remote_copy(
            src_ref=src.at[:, pl.ds(0, BLOCK)], dst_ref=dst, send_sem=tok_send.at[k], recv_sem=tok_recv.at[k],
            device_id={"seq": before}, device_id_type=MESH,
        )
        copy.start()
        tok_copies.append(copy)

    eye = shift_matrix(HD, HD, 0)

    for load in loads:
        load.wait()
    for k in range(SLOTS):
        recv[k] = store_ref[own_ids[k]]

    def turn_states(i, c):
        st[i] = nt(eye, s_ref[i]).astype(bf16)
        return c

    lax.fori_loop(0, seqs * groups, turn_states, 0)

    for k, (low, high, distance) in enumerate(parts):
        rows = ids_in.at[pl.ds(low, high - low)]
        pltpu.make_async_copy(rows, rows, ids_recv.at[k]).wait()
        to_scalar = pltpu.make_async_copy(rows, ids_s.at[pl.ds(low, high - low)], loc_sem.at[k])
        to_scalar.start()
        to_scalar.wait()

        def send_items(p, c, distance=distance):
            for k in range(SLOTS):
                send[SLOTS * p + k] = store_ref[ids_s[p, 0, SLOTS * p + k]]
            pltpu.make_async_remote_copy(
                src_ref=send.at[pl.ds(SLOTS * p, SLOTS)], dst_ref=recv.at[pl.ds(SLOTS * p, SLOTS)],
                send_sem=data_send, recv_sem=data_recv.at[p], device_id=ring(distance(p, members)), device_id_type=MESH,
            ).start()
            return c

        lax.fori_loop(low, high, send_items, 0)

    for copy in tok_copies:
        copy.wait()
    last = (me < members - 1).astype(f32)
    first = (me > 0).astype(f32)
    for b in range(seqs):
        qn[b] = (qn[b].astype(f32) * last).astype(bf16)
        gn[b] = (gn[b].astype(f32) * last).astype(bf16)
    take = shift_matrix(BLOCK, 2 * BLOCK, BLOCK - 1)
    for b in range(seqs):
        for g in range(groups):
            i = b * groups + g
            for src, nxt, flat, turned in ((q_ref, qn, qb, qt), (g_ref, gn, gb, gt)):
                if g < groups - 1:
                    rows = src[b, pl.ds(BLOCK * g, 2 * BLOCK)]
                else:
                    rows = jnp.concatenate([src[b, pl.ds(BLOCK * g, BLOCK)], nxt[b]], axis=0)
                block = nn(take, rows).astype(bf16)
                flat[i] = block
                turned[i] = nt(eye, block).astype(bf16)

    def encode(slot, row):
        block = slot_block[slot]
        rows = recv[slot]
        scores = nt(s_ref[block], rows) * scale
        top = jnp.max(scores, axis=0, keepdims=True)
        raised = jnp.exp(scores - top)
        weights = raised / jnp.sum(raised, axis=0, keepdims=True)
        total = nn(st[block], weights.astype(bf16)) + nt(eye, rows)
        wts[slot] = weights
        summed[slot] = total
        ukeys[slot] = total.astype(bf16)
        squares[row[0], 0, pl.ds(row[1], 1), :] = jnp.sum(total * total, axis=0, keepdims=True)

    chunks = members // chunk
    rows_chunk = chunk * SLOTS

    def send_squares(c):
        def one(q, x):
            pltpu.make_async_remote_copy(
                src_ref=squares.at[c, 0], dst_ref=squares.at[c, q], send_sem=sq_send, recv_sem=sq_recv.at[c],
                device_id=plane(q), device_id_type=MESH,
            ).start()
            return x
        lax.fori_loop(1, peers, one, 0)

    for k in range(SLOTS):
        encode(k, (0, k))

    def encode_chunk(c, x):
        def one(p, y):
            pltpu.make_async_copy(
                recv.at[pl.ds(SLOTS * p, SLOTS)], recv.at[pl.ds(SLOTS * p, SLOTS)], data_recv.at[p]
            ).wait()
            for k in range(SLOTS):
                encode(SLOTS * p + k, (c, SLOTS * (p - c * chunk) + k))
            return y
        lax.fori_loop(jnp.maximum(c * chunk, 1), (c + 1) * chunk, one, 0)
        send_squares(c)
        return x

    lax.fori_loop(0, chunks, encode_chunk, 0)

    def raw_scores(b, g):
        i = b * groups + g
        item = (g * seqs + b) * NBR
        keys = jnp.concatenate([ukeys[item_slot[item + n]] for n in range(NBR)], axis=1)
        kblk[i] = keys
        sraw[i] = nn(qb[i], keys)
        wraw[i] = nn(gb[i], keys)

    order = [groups - 1] + list(range(groups - 1))
    for g in order:
        for b in range(seqs):
            raw_scores(b, g)

    def finish_squares(c, x):
        pltpu.make_async_copy(
            squares.at[c, pl.ds(1, peers - 1)], squares.at[c, pl.ds(1, peers - 1)], sq_recv.at[c]
        ).wait()
        total = jnp.sum(squares[c], axis=0)
        inv[pl.ds(rows_chunk * c, rows_chunk), :] = lax.rsqrt(total / width + norm_eps)
        return x

    lax.fori_loop(0, chunks, finish_squares, 0)

    def attend(b, g):
        i = b * groups + g
        item = (g * seqs + b) * NBR
        slots = [item_slot[item + n] for n in range(NBR)]
        scaled = jnp.concatenate([inv[pl.ds(slot, 1), :] for slot in slots], axis=1)
        keys = kblk[i]
        scores = sraw[i] * (scaled * scale)
        raised = jnp.exp(scores - jnp.max(scores, axis=1, keepdims=True))
        weights = raised / jnp.sum(raised, axis=1, keepdims=True)
        atb[g + 1, b] = nt((weights * scaled).astype(bf16), keys).astype(bf16)
        wgrad = wraw[i] * scaled
        sgrad = weights * (wgrad - jnp.sum(weights * wgrad, axis=1, keepdims=True))
        qgb[g + 1, b] = (scale * nt((sgrad * scaled).astype(bf16), keys)).astype(bf16)
        grad = (nn(gt[i], weights.astype(bf16)) + scale * nn(qt[i], sgrad.astype(bf16))).astype(bf16)
        kgrad[i] = grad
        totals = jnp.concatenate([summed[slot] for slot in slots], axis=1)
        inner = scaled * jnp.sum(grad.astype(f32) * totals, axis=0, keepdims=True)
        for n in range(NBR):
            proj[g, 0, pl.ds(NBR * b + n, 1), :] = inner[:, n * NLEN:(n + 1) * NLEN]

    def encode_grad(b, g):
        i = b * groups + g
        item = (g * seqs + b) * NBR
        total = None
        for n in range(NBR):
            slot = item_slot[item + n]
            scaled = inv[pl.ds(slot, 1), :]
            row = jnp.sum(proj[g, :, NBR * b + n, :], axis=0, keepdims=True) / width
            grad = kgrad[i, :, pl.ds(n * NLEN, NLEN)].astype(f32)
            sgrad = (grad * scaled - summed[slot] * (scaled * scaled * row)).astype(bf16)
            weights = wts[slot]
            wgrad = nn(s_ref[i], sgrad)
            slow = (weights * (wgrad - jnp.sum(weights * wgrad, axis=0, keepdims=True))).astype(bf16)
            term = nt(weights.astype(bf16), sgrad) + scale * nn(slow, recv[slot])
            term = term.astype(bf16).astype(f32)
            total = term if total is None else total + term
        sg_ref[b, pl.ds(g * BLOCK, BLOCK)] = total.astype(bf16)

    o_copies = []
    for g in order:
        for b in range(seqs):
            attend(b, g)
        if g == groups - 1:
            for k, buf in enumerate((atb, qgb)):
                copy = pltpu.make_async_remote_copy(
                    src_ref=buf.at[groups], dst_ref=buf.at[0], send_sem=o_send.at[k], recv_sem=o_recv.at[k],
                    device_id={"seq": after}, device_id_type=MESH,
                )
                copy.start()
                o_copies.append(copy)

        def send_proj(q, x, g=g):
            pltpu.make_async_remote_copy(
                src_ref=proj.at[g, 0], dst_ref=proj.at[g, q], send_sem=pr_send, recv_sem=pr_recv.at[g],
                device_id=plane(q), device_id_type=MESH,
            ).start()
            return x

        lax.fori_loop(1, peers, send_proj, 0)

    for g in order:
        pltpu.make_async_copy(
            proj.at[g, pl.ds(1, peers - 1)], proj.at[g, pl.ds(1, peers - 1)], pr_recv.at[g]
        ).wait()
        for b in range(seqs):
            encode_grad(b, g)

    for copy in o_copies:
        copy.wait()
    back = shift_matrix(BLOCK, 2 * BLOCK, 1)
    for buf, out in ((atb, att_ref), (qgb, qg_ref)):
        for b in range(seqs):
            buf[0, b] = (buf[0, b].astype(f32) * first).astype(bf16)
        for g in range(groups):
            for b in range(seqs):
                rows = jnp.concatenate([buf[g, b], buf[g + 1, b]], axis=0)
                out[b, pl.ds(g * BLOCK, BLOCK)] = nn(back, rows).astype(bf16)

    pltpu.make_async_copy(ids_in.at[pl.ds(1, members - 1)], ids_in.at[pl.ds(1, members - 1)], ids_send).wait()
    pltpu.make_async_copy(
        send.at[pl.ds(SLOTS, SLOTS * (members - 1))], send.at[pl.ds(SLOTS, SLOTS * (members - 1))], data_send
    ).wait()
    whole = squares.at[pl.ds(0, chunks), pl.ds(1, peers - 1)]
    pltpu.make_async_copy(whole, whole, sq_send).wait()
    whole = proj.at[pl.ds(0, groups), pl.ds(1, peers - 1)]
    pltpu.make_async_copy(whole, whole, pr_send).wait()


def on_device(members, ntp, ndp, queries, block_states, grad_out, store, owners, entries):
    seqs, rows, columns = queries.shape
    groups = rows // BLOCK
    blocks = seqs * groups
    items = blocks * NBR
    peers = ntp * ndp
    me = lax.axis_index("seq")
    flat_owner = owners.reshape(items)
    flat_entry = entries.reshape(items)

    distance = (me - flat_owner + members) % members
    half, reach = members // 2, near_places(members) // 2
    step = distance - half
    place = near_places(members) + jnp.where(step > 0, 2 * step + 1, jnp.where(step == 0, 1, -2 * step))
    place = jnp.where(distance <= reach, 2 * distance - 1, place)
    place = jnp.where(distance >= members - reach, 2 * (members - distance), place)
    place = jnp.where(distance == 0, 0, place)
    number = jnp.arange(items, dtype=jnp.int32)
    same = (flat_owner[:, None] == flat_owner[None, :]) & (number[None, :] < number[:, None])
    item_slot = place * SLOTS + jnp.sum(same.astype(jnp.int32), axis=1)
    cells = jnp.arange(members * SLOTS, dtype=jnp.int32)
    held = cells[:, None] == item_slot[None, :]
    slot_ids = jnp.sum(jnp.where(held, flat_entry[None, :], 0), axis=1)
    pair = number // NBR
    block_index = (pair % seqs) * groups + pair // seqs
    slot_block = jnp.sum(jnp.where(held, block_index[None, :], 0), axis=1)
    ids_row = jnp.pad(slot_ids, (0, 128 - members * SLOTS)).reshape(1, 128)

    chunk = max(1, members // 4)
    chunks = members // chunk
    vmem, smem = pltpu.VMEM, pltpu.SMEM
    dma = pltpu.SemaphoreType.DMA
    in_vmem = pl.BlockSpec(memory_space=vmem)
    in_smem = pl.BlockSpec(memory_space=smem)
    out = jax.ShapeDtypeStruct((seqs, rows, columns), bf16)
    attended, query_grad, state_grad = pl.pallas_call(
        functools.partial(kernel, members, ntp, ndp, seqs, groups, chunk),
        out_shape=(out, out, out),
        in_specs=[in_smem] * 3 + [in_vmem] + [pl.BlockSpec(memory_space=pltpu.HBM)] * 4,
        out_specs=(in_vmem,) * 3,
        scratch_shapes=[
            vmem(queries.shape, bf16),
            vmem(queries.shape, bf16),
            vmem((blocks, BLOCK, columns), bf16),
            vmem(store.shape, bf16),
            vmem((members, 1, 128), jnp.int32),
            smem((members, 1, 128), jnp.int32),
            vmem((members * SLOTS, NLEN, HD), bf16),
            vmem((members * SLOTS, NLEN, HD), bf16),
            vmem((members * SLOTS, HD, NLEN), f32),
            vmem((members * SLOTS, HD, NLEN), bf16),
            vmem((blocks, BLOCK, NBR * NLEN), f32),
            vmem((blocks, BLOCK, NBR * NLEN), f32),
            vmem((members * SLOTS, BLOCK, NLEN), f32),
            vmem((chunks, peers, chunk * SLOTS, NLEN), f32),
            vmem((members * SLOTS, NLEN), f32),
            vmem((seqs, BLOCK, HD), bf16),
            vmem((seqs, BLOCK, HD), bf16),
            vmem((blocks, BLOCK, HD), bf16),
            vmem((blocks, BLOCK, HD), bf16),
            vmem((blocks, HD, BLOCK), bf16),
            vmem((blocks, HD, BLOCK), bf16),
            vmem((blocks, HD, BLOCK), bf16),
            vmem((blocks, HD, NBR * NLEN), bf16),
            vmem((groups + 1, seqs, BLOCK, HD), bf16),
            vmem((groups + 1, seqs, BLOCK, HD), bf16),
            vmem((blocks, HD, NBR * NLEN), bf16),
            vmem((groups, peers, seqs * NBR, NLEN), f32),
            dma((4,)), dma, dma((2,)), dma((2,)), dma((2,)), dma((2,)),
            dma, dma((members,)), dma, dma((chunks,)), dma, dma((groups,)),
            dma((2,)), dma((2,)),
        ],
        compiler_params=pltpu.CompilerParams(
            collective_id=0, has_side_effects=True, vmem_limit_bytes=48 * 1024 * 1024
        ),
    )(
        item_slot, slot_block, slot_ids, ids_row, queries, grad_out,
        block_states.reshape(blocks, BLOCK, columns), store,
    )
    return attended, query_grad, state_grad


def solution(mesh):
    members, ntp, ndp = (mesh.shape[a] for a in ("seq", "tp", "dp"))
    rows = P(None, "seq", ("tp", "dp"))
    return jax.shard_map(
        functools.partial(on_device, members, ntp, ndp),
        mesh=mesh,
        in_specs=(rows, rows, rows, P("seq", None, ("tp", "dp")), P("seq", None, None), P("seq", None, None)),
        out_specs=(rows, rows, rows),
        check_vma=False,
    )
```

```python
import functools

import jax
import jax.numpy as jnp
from jax import lax
from jax.experimental import pallas as pl
from jax.experimental.pallas import tpu as pltpu
from jax.sharding import PartitionSpec as P

HD = 128
BLOCK = 64
NLEN = 128
NBR = 2
SLOTS = 2
norm_eps = 1e-06
MESH = pl.DeviceIdType.MESH
f32 = jnp.float32
bf16 = jnp.bfloat16


def near_places(members):
    return min(10, (members // 4) * 2)


def near_distance(place, members):
    return members + ((place + 1) // 2) * (1 - 2 * ((place + 1) % 2))


def far_distance(place, members):
    step = place - 1 - near_places(members)
    return members // 2 + ((step + 1) // 2) * (1 - 2 * (step % 2))


def owner_place(distance, members):
    reach = near_places(members) // 2
    step = distance - members // 2
    place = near_places(members) + jnp.where(step > 0, 2 * step + 1, jnp.where(step == 0, 1, -2 * step))
    place = jnp.where(distance <= reach, 2 * distance - 1, place)
    place = jnp.where(distance >= members - reach, 2 * (members - distance), place)
    return jnp.where(distance == 0, 0, place)


def nn(a, b):
    return lax.dot_general(a, b, (((1,), (0,)), ((), ())), preferred_element_type=f32)


def nt(a, b):
    return lax.dot_general(a, b, (((1,), (1,)), ((), ())), preferred_element_type=f32)


def shift_matrix(rows, columns, offset):
    i = lax.broadcasted_iota(jnp.int32, (rows, columns), 0)
    j = lax.broadcasted_iota(jnp.int32, (rows, columns), 1)
    return (j == i + offset).astype(f32).astype(bf16)


def kernel(
    members, ntp, ndp, seqs, groups, chunks,
    owners_hbm, entries_hbm, q_hbm, g_hbm, s_hbm, store_hbm,
    att_ref, qg_ref, sg_ref,
    owner_s, entry_s, slots, plan, ids_ref, slot_s, plan_s,
    q_ref, g_ref, s_ref, store_ref, ids_in, ids_s, send, recv, summed, ukeys, sraw, wraw, wts, squares, inv, qn, gn, qb, gb, qt, gt, st, kblk, atb, qgb, kgrad, proj,
    plan_sem, in_sem, ids_send, ids_recv, loc_sem, tok_send, tok_recv, data_send, data_recv, sq_send, sq_recv, pr_send, pr_recv,
    o_send, o_recv,
):
    me = lax.axis_index("seq")
    tp = lax.axis_index("tp")
    dp = lax.axis_index("dp")
    peers = ntp * ndp
    scale = HD ** (-0.5)
    width = HD * peers
    after = lax.rem(me + 1, members)
    before = lax.rem(me + members - 1, members)

    def ring(distance):
        return {"seq": lax.rem(me + distance, members)}

    def plane(q):
        return {"tp": lax.rem(tp + q // ndp, ntp), "dp": lax.rem(dp + q % ndp, ndp)}

    barrier = pltpu.get_barrier_semaphore()

    def greet_ring(d, c):
        pl.semaphore_signal(barrier, inc=1, device_id=ring(d), device_id_type=MESH)
        return c

    def greet_plane(q, c):
        pl.semaphore_signal(barrier, inc=1, device_id=plane(q), device_id_type=MESH)
        return c

    lax.fori_loop(1, members, greet_ring, 0)
    lax.fori_loop(1, peers, greet_plane, 0)
    tables = []
    for k, (src, dst) in enumerate(((owners_hbm, owner_s), (entries_hbm, entry_s))):
        table = pltpu.make_async_copy(src, dst, plan_sem.at[k])
        table.start()
        tables.append(table)
    loads = []
    for k, (src, dst) in enumerate(((store_hbm, store_ref), (s_hbm, s_ref), (q_hbm, q_ref), (g_hbm, g_ref))):
        load = pltpu.make_async_copy(src, dst, in_sem.at[k])
        load.start()
        loads.append(load)

    for table in tables:
        table.wait()
    items = groups * NBR * seqs
    row = lax.broadcasted_iota(jnp.int32, (items, 128), 0)
    lane = lax.broadcasted_iota(jnp.int32, (items, 128), 1)
    owner = jnp.zeros((items, 128), jnp.int32)
    entry = jnp.zeros((items, 128), jnp.int32)
    rank = jnp.zeros((items, 128), jnp.int32)
    flat = [(g, n, b) for g in range(groups) for n in range(NBR) for b in range(seqs)]
    for i, at in enumerate(flat):
        owner = jnp.where(row == i, owner_s[at], owner)
        entry = jnp.where(row == i, entry_s[at], entry)
    for i, at in enumerate(flat):
        rank = jnp.where((row > i) & (owner == owner_s[at]), rank + 1, rank)
    slot = owner_place(lax.rem(me - owner + members, members), members) * SLOTS + rank
    slot = jnp.clip(slot, 0, members * SLOTS - 1)
    group = row // (NBR * seqs)
    held = slot == lane
    slots[...] = slot
    wanted = jnp.sum(jnp.where(held, entry, 0), axis=0, keepdims=True)
    ids_ref[...] = jnp.clip(wanted, 0, store_ref.shape[0] - 1)
    plan[0:1, :] = ids_ref[...]
    whose = jnp.sum(jnp.where(held, (row % seqs) * groups + group, 0), axis=0, keepdims=True)
    plan[1:2, :] = jnp.clip(whose, 0, seqs * groups - 1)
    scalars = []
    for k, (src, dst) in enumerate(((plan, plan_s), (slots, slot_s))):
        scalar = pltpu.make_async_copy(src, dst, plan_sem.at[2 + k])
        scalar.start()
        scalars.append(scalar)
    pl.semaphore_wait(barrier, members - 1 + peers - 1)

    near = near_places(members)
    parts = ((1, near + 1, near_distance), (near + 1, members, far_distance))
    for k, (low, high, distance) in enumerate(parts):
        def send_ids(p, c, k=k, distance=distance):
            pltpu.make_async_remote_copy(
                src_ref=ids_ref, dst_ref=ids_in.at[p], send_sem=ids_send, recv_sem=ids_recv.at[k],
                device_id=ring(2 * members - distance(p, members)), device_id_type=MESH,
            ).start()
            return c

        lax.fori_loop(low, high, send_ids, 0)
    tok_copies = []
    for k, (src, dst) in enumerate(((q_hbm, qn), (g_hbm, gn))):
        copy = pltpu.make_async_remote_copy(
            src_ref=src.at[:, pl.ds(0, BLOCK)], dst_ref=dst, send_sem=tok_send.at[k], recv_sem=tok_recv.at[k],
            device_id={"seq": before}, device_id_type=MESH,
        )
        copy.start()
        tok_copies.append(copy)

    eye = shift_matrix(HD, HD, 0)

    for load in loads + scalars:
        load.wait()
    for k in range(SLOTS):
        recv[k] = store_ref[plan_s[0, k]]

    def turn_states(i, c):
        st[i] = nt(eye, s_ref[i]).astype(bf16)
        return c

    lax.fori_loop(0, seqs * groups, turn_states, 0)

    for k, (low, high, distance) in enumerate(parts):
        rows = ids_in.at[pl.ds(low, high - low)]
        pltpu.make_async_copy(rows, rows, ids_recv.at[k]).wait()
        to_scalar = pltpu.make_async_copy(rows, ids_s.at[pl.ds(low, high - low)], loc_sem.at[k])
        to_scalar.start()
        to_scalar.wait()

        def send_items(p, c, distance=distance):
            for k in range(SLOTS):
                send[SLOTS * p + k] = store_ref[ids_s[p, 0, SLOTS * p + k]]
            pltpu.make_async_remote_copy(
                src_ref=send.at[pl.ds(SLOTS * p, SLOTS)], dst_ref=recv.at[pl.ds(SLOTS * p, SLOTS)],
                send_sem=data_send, recv_sem=data_recv.at[p], device_id=ring(distance(p, members)), device_id_type=MESH,
            ).start()
            return c

        lax.fori_loop(low, high, send_items, 0)

    for copy in tok_copies:
        copy.wait()
    last = (me < members - 1).astype(f32)
    first = (me > 0).astype(f32)
    for b in range(seqs):
        qn[b] = (qn[b].astype(f32) * last).astype(bf16)
        gn[b] = (gn[b].astype(f32) * last).astype(bf16)
    take = shift_matrix(BLOCK, 2 * BLOCK, BLOCK - 1)
    for b in range(seqs):
        for g in range(groups):
            i = b * groups + g
            for src, nxt, flat, turned in ((q_ref, qn, qb, qt), (g_ref, gn, gb, gt)):
                if g < groups - 1:
                    rows = src[b, pl.ds(BLOCK * g, 2 * BLOCK)]
                else:
                    rows = jnp.concatenate([src[b, pl.ds(BLOCK * g, BLOCK)], nxt[b]], axis=0)
                block = nn(take, rows).astype(bf16)
                flat[i] = block
                turned[i] = nt(eye, block).astype(bf16)

    def encode(slot):
        block = plan_s[1, slot]
        rows = recv[slot]
        scores = nt(s_ref[block], rows) * scale
        top = jnp.max(scores, axis=0, keepdims=True)
        raised = jnp.exp(scores - top)
        weights = raised / jnp.sum(raised, axis=0, keepdims=True)
        total = nn(st[block], weights.astype(bf16)) + nt(eye, rows)
        wts[slot] = weights
        summed[slot] = total
        ukeys[slot] = total.astype(bf16)
        squares[0, pl.ds(slot, 1), :] = jnp.sum(total * total, axis=0, keepdims=True)

    def send_squares(c, low, high):
        rows = pl.ds(SLOTS * low, SLOTS * (high - low))

        def one(q, x):
            pltpu.make_async_remote_copy(
                src_ref=squares.at[0, rows], dst_ref=squares.at[q, rows], send_sem=sq_send, recv_sem=sq_recv.at[c],
                device_id=plane(q), device_id_type=MESH,
            ).start()
            return x

        lax.fori_loop(1, peers, one, 0)

    for k in range(SLOTS):
        encode(k)

    def take_place(p, x):
        rows = recv.at[pl.ds(SLOTS * p, SLOTS)]
        pltpu.make_async_copy(rows, rows, data_recv.at[p]).wait()
        for k in range(SLOTS):
            encode(SLOTS * p + k)
        return x

    for c, (low, high) in enumerate(chunks):
        lax.fori_loop(max(low, 1), high, take_place, 0)
        send_squares(c, low, high)

    def raw_scores(b, g):
        i = b * groups + g
        item = g * NBR * seqs + b
        keys = jnp.concatenate([ukeys[slot_s[item + n * seqs, 0]] for n in range(NBR)], axis=1)
        kblk[i] = keys
        sraw[i] = nn(qb[i], keys)
        wraw[i] = nn(gb[i], keys)

    order = [groups - 1] + list(range(groups - 1))
    for g in order:
        for b in range(seqs):
            raw_scores(b, g)

    for c, (low, high) in enumerate(chunks):
        rows = pl.ds(SLOTS * low, SLOTS * (high - low))
        sums = squares.at[pl.ds(1, peers - 1), rows]
        pltpu.make_async_copy(sums, sums, sq_recv.at[c]).wait()
        inv[rows, :] = lax.rsqrt(jnp.sum(squares[:, rows, :], axis=0) / width + norm_eps)

    def attend(b, g):
        i = b * groups + g
        item = g * NBR * seqs + b
        slots = [slot_s[item + n * seqs, 0] for n in range(NBR)]
        scaled = jnp.concatenate([inv[pl.ds(slot, 1), :] for slot in slots], axis=1)
        keys = kblk[i]
        scores = sraw[i] * (scaled * scale)
        raised = jnp.exp(scores - jnp.max(scores, axis=1, keepdims=True))
        weights = raised / jnp.sum(raised, axis=1, keepdims=True)
        atb[g + 1, b] = nt((weights * scaled).astype(bf16), keys).astype(bf16)
        wgrad = wraw[i] * scaled
        sgrad = weights * (wgrad - jnp.sum(weights * wgrad, axis=1, keepdims=True))
        qgb[g + 1, b] = (scale * nt((sgrad * scaled).astype(bf16), keys)).astype(bf16)
        grad = (nn(gt[i], weights.astype(bf16)) + scale * nn(qt[i], sgrad.astype(bf16))).astype(bf16)
        kgrad[i] = grad
        totals = jnp.concatenate([summed[slot] for slot in slots], axis=1)
        inner = scaled * jnp.sum(grad.astype(f32) * totals, axis=0, keepdims=True)
        for n in range(NBR):
            proj[g, 0, pl.ds(NBR * b + n, 1), :] = inner[:, n * NLEN:(n + 1) * NLEN]

    def encode_grad(b, g):
        i = b * groups + g
        item = g * NBR * seqs + b
        total = None
        for n in range(NBR):
            slot = slot_s[item + n * seqs, 0]
            scaled = inv[pl.ds(slot, 1), :]
            row = jnp.sum(proj[g, :, NBR * b + n, :], axis=0, keepdims=True) / width
            grad = kgrad[i, :, pl.ds(n * NLEN, NLEN)].astype(f32)
            sgrad = (grad * scaled - summed[slot] * (scaled * scaled * row)).astype(bf16)
            weights = wts[slot]
            wgrad = nn(s_ref[i], sgrad)
            slow = (weights * (wgrad - jnp.sum(weights * wgrad, axis=0, keepdims=True))).astype(bf16)
            term = nt(weights.astype(bf16), sgrad) + scale * nn(slow, recv[slot])
            term = term.astype(bf16).astype(f32)
            total = term if total is None else total + term
        sg_ref[b, pl.ds(g * BLOCK, BLOCK)] = total.astype(bf16)

    o_copies = []
    for g in order:
        for b in range(seqs):
            attend(b, g)
        if g == groups - 1:
            for k, buf in enumerate((atb, qgb)):
                copy = pltpu.make_async_remote_copy(
                    src_ref=buf.at[groups], dst_ref=buf.at[0], send_sem=o_send.at[k], recv_sem=o_recv.at[k],
                    device_id={"seq": after}, device_id_type=MESH,
                )
                copy.start()
                o_copies.append(copy)

        def send_proj(q, x, g=g):
            pltpu.make_async_remote_copy(
                src_ref=proj.at[g, 0], dst_ref=proj.at[g, q], send_sem=pr_send, recv_sem=pr_recv.at[g],
                device_id=plane(q), device_id_type=MESH,
            ).start()
            return x

        lax.fori_loop(1, peers, send_proj, 0)

    back = shift_matrix(BLOCK, 2 * BLOCK, 1)

    def token_order(g):
        for buf, out in ((atb, att_ref), (qgb, qg_ref)):
            for b in range(seqs):
                rows = jnp.concatenate([buf[g, b], buf[g + 1, b]], axis=0)
                out[b, pl.ds(g * BLOCK, BLOCK)] = nn(back, rows).astype(bf16)

    for g in range(1, groups):
        token_order(g)

    for g in order:
        pltpu.make_async_copy(
            proj.at[g, pl.ds(1, peers - 1)], proj.at[g, pl.ds(1, peers - 1)], pr_recv.at[g]
        ).wait()
        for b in range(seqs):
            encode_grad(b, g)

    for copy in o_copies:
        copy.wait()
    for buf in (atb, qgb):
        for b in range(seqs):
            buf[0, b] = (buf[0, b].astype(f32) * first).astype(bf16)
    token_order(0)

    pltpu.make_async_copy(ids_in.at[pl.ds(1, members - 1)], ids_in.at[pl.ds(1, members - 1)], ids_send).wait()
    pltpu.make_async_copy(
        send.at[pl.ds(SLOTS, SLOTS * (members - 1))], send.at[pl.ds(SLOTS, SLOTS * (members - 1))], data_send
    ).wait()
    whole = squares.at[pl.ds(1, peers - 1)]
    pltpu.make_async_copy(whole, whole, sq_send).wait()
    whole = proj.at[pl.ds(0, groups), pl.ds(1, peers - 1)]
    pltpu.make_async_copy(whole, whole, pr_send).wait()


def on_device(members, ntp, ndp, queries, block_states, grad_out, store, owners, entries):
    seqs, rows, columns = queries.shape
    groups = rows // BLOCK
    blocks = seqs * groups
    items = blocks * NBR
    peers = ntp * ndp
    bounds = sorted({0, members // 4, members // 2, members * 3 // 4, members * 7 // 8, members * 15 // 16, members})
    chunks = list(zip(bounds[:-1], bounds[1:]))
    vmem, smem = pltpu.VMEM, pltpu.SMEM
    dma = pltpu.SemaphoreType.DMA
    out = jax.ShapeDtypeStruct((seqs, rows, columns), bf16)
    attended, query_grad, state_grad = pl.pallas_call(
        functools.partial(kernel, members, ntp, ndp, seqs, groups, chunks),
        out_shape=(out, out, out),
        in_specs=[pl.BlockSpec(memory_space=pltpu.HBM)] * 6,
        out_specs=(pl.BlockSpec(memory_space=vmem),) * 3,
        scratch_shapes=[
            smem((groups, NBR, seqs), jnp.int32),
            smem((groups, NBR, seqs), jnp.int32),
            vmem((items, 128), jnp.int32),
            vmem((8, 128), jnp.int32),
            vmem((1, 128), jnp.int32),
            smem((items, 128), jnp.int32),
            smem((8, 128), jnp.int32),
            vmem(queries.shape, bf16),
            vmem(queries.shape, bf16),
            vmem((blocks, BLOCK, columns), bf16),
            vmem(store.shape, bf16),
            vmem((members, 1, 128), jnp.int32),
            smem((members, 1, 128), jnp.int32),
            vmem((members * SLOTS, NLEN, HD), bf16),
            vmem((members * SLOTS, NLEN, HD), bf16),
            vmem((members * SLOTS, HD, NLEN), f32),
            vmem((members * SLOTS, HD, NLEN), bf16),
            vmem((blocks, BLOCK, NBR * NLEN), f32),
            vmem((blocks, BLOCK, NBR * NLEN), f32),
            vmem((members * SLOTS, BLOCK, NLEN), f32),
            vmem((peers, members * SLOTS, NLEN), f32),
            vmem((members * SLOTS, NLEN), f32),
            vmem((seqs, BLOCK, HD), bf16),
            vmem((seqs, BLOCK, HD), bf16),
            vmem((blocks, BLOCK, HD), bf16),
            vmem((blocks, BLOCK, HD), bf16),
            vmem((blocks, HD, BLOCK), bf16),
            vmem((blocks, HD, BLOCK), bf16),
            vmem((blocks, HD, BLOCK), bf16),
            vmem((blocks, HD, NBR * NLEN), bf16),
            vmem((groups + 1, seqs, BLOCK, HD), bf16),
            vmem((groups + 1, seqs, BLOCK, HD), bf16),
            vmem((blocks, HD, NBR * NLEN), bf16),
            vmem((groups, peers, seqs * NBR, NLEN), f32),
            dma((4,)), dma((4,)), dma, dma((2,)), dma((2,)), dma((2,)), dma((2,)),
            dma, dma((members,)), dma, dma((len(chunks),)), dma, dma((groups,)),
            dma((2,)), dma((2,)),
        ],
        compiler_params=pltpu.CompilerParams(
            collective_id=0, has_side_effects=True, vmem_limit_bytes=62690000
        ),
    )(
        jnp.transpose(owners, (0, 2, 1)), jnp.transpose(entries, (0, 2, 1)), queries, grad_out,
        block_states.reshape(blocks, BLOCK, columns), store,
    )
    def hand_on(a_in, q_in, s_in, a_out, q_out, s_out, sems):
        copies = []
        for k, (src, dst) in enumerate(((a_in, a_out), (q_in, q_out), (s_in, s_out))):
            copy = pltpu.make_async_copy(src, dst, sems.at[k])
            copy.start()
            copies.append(copy)
        for copy in copies:
            copy.wait()

    hbm = pl.BlockSpec(memory_space=pltpu.HBM)
    return pl.pallas_call(
        hand_on, out_shape=(out, out, out), in_specs=[pl.BlockSpec(memory_space=vmem)] * 3, out_specs=(hbm,) * 3, scratch_shapes=[dma((3,))],
    )(attended, query_grad, state_grad)


def solution(mesh):
    members, ntp, ndp = (mesh.shape[a] for a in ("seq", "tp", "dp"))
    rows = P(None, "seq", ("tp", "dp"))
    return jax.shard_map(
        functools.partial(on_device, members, ntp, ndp),
        mesh=mesh,
        in_specs=(rows, rows, rows, P("seq", None, ("tp", "dp")), P("seq", None, None), P("seq", None, None)),
        out_specs=(rows, rows, rows),
        check_vma=False,
    )
```
